32 devices in a mesh: real: 2 (over y), col: 8 (over z, x), row: 2 (over core).
Axes of the slice: x: 2, y: 2, z: 4, core: 2. Of those that a mesh axis runs over, the one named last changes fastest.
Arguments:
- theta: bfloat16 [512, 16384], P(('real', 'row'), 'col'), parts along dimension 0, may hold values from -6 to 6
- signs: int32 [32768], P(('real', 'col')), parts along dimension 0, may hold values from -1 to 1, as said below
- kept: int32 [1024], replicated, may hold values from 0 to 16383, as said below
Outputs:
- gram: float32 [4, 8, 16, 256], P(('real', 'row'), 'col'), parts along dimension 0
The draws below stay inside these ranges and needn't reach their ends.
There are 2 independent parts, one for each index of `real`. The reference program is written for one: setup_inputs(seed, part) draws one part's arguments, and reference() takes and returns one part's arrays. A program takes and returns all parts, laid end to end along the dimension named above; an argument that names none is the same for every part. Nothing has to cross between parts.
Inputs may be any that keep to these rules, and one draw needn't show every extreme that they name: `signs`: each entry is -1 or 1. `kept`: 1024 distinct column indices.
All inputs are finite; a program needn't handle non-finite values.
Results may differ from the reference program's by a relative error of at most 0.0036.
Values may be sent and summed in bfloat16 or wider, within the bound.
A program may use at most 64 MiB of HBM per device.

```python
import jax
import jax.numpy as jnp
from jax import lax

SIDE = 128
N = 16384
KEEP = 1024
ROW_DEV = 16
ROWS = 256
N_COL = 8
N_ROW = 2


def draw_signs(key, part):
    return (2 * jax.random.randint(jax.random.fold_in(key, 11), (N,), 0, 2) - 1).astype(jnp.int32)


def draw_kept(key, part):
    middle = 1 + jax.random.permutation(jax.random.fold_in(key, 23), N - 2)[:KEEP - 2]
    ends = jnp.array([0, N - 1], dtype=jnp.int32)
    whole = jnp.concatenate([ends, middle.astype(jnp.int32)])
    order = jax.random.permutation(jax.random.fold_in(key, 29), KEEP)
    return whole[order].astype(jnp.int32)


def level_of(own_key, extent, cuts, low, top_value):
    loudness = 1.0
    for dim, parts in cuts:
        heights = jax.random.uniform(jax.random.fold_in(jax.random.fold_in(own_key, 6), dim), (parts,), jnp.float32, low / len(cuts), top_value / len(cuts))
        loudness = loudness * jnp.repeat(jnp.exp(heights), extent[dim] // parts).reshape((-1,) + (1,) * (len(extent) - 1 - dim))
    return loudness


def bell_draw(own_key, extent, spread, reach, cuts=(), kind=jnp.bfloat16):
    gain = level_of(own_key, extent, cuts, -0.22, 0.18) if cuts else 1.0
    values = jax.random.normal(own_key, extent, jnp.float32) * spread * gain
    return jnp.minimum(jnp.maximum(values, -reach), reach).astype(kind)


def setup_inputs(seed: int = 0, part: int = 0) -> dict:
    arg_keys = jax.random.split(jax.random.key(seed), 4)
    part_keys = jax.random.split(jax.random.fold_in(arg_keys[3], part), 4)
    theta = bell_draw(part_keys[0], (ROWS, N), 1.0, 6.0, ((0, 2), (1, 8)))
    signs = draw_signs(jax.random.fold_in(jax.random.fold_in(arg_keys[3], part), 71), part)
    kept = draw_kept(jax.random.fold_in(arg_keys[3], 71), part)
    return {"theta": theta, "signs": signs, "kept": kept}


def hadamard(order, dtype):
    indices = jnp.arange(order, dtype=jnp.int32)
    common = indices[:, None] & indices[None, :]
    parity = jnp.zeros((order, order), jnp.int32)
    for position in range(order.bit_length() - 1):
        parity = parity ^ ((common >> position) & 1)
    return (1 - 2 * parity).astype(dtype)


def reference(theta, signs, kept):
    scaled = theta * signs.astype(jnp.bfloat16)[None, :]
    flat = scaled.astype(jnp.float32).reshape(ROWS * SIDE, SIDE)
    table = hadamard(SIDE, jnp.float32)
    inner = jnp.dot(flat, table, precision=lax.Precision.HIGHEST).reshape(ROWS, SIDE, SIDE)
    outer = jnp.einsum("rak,aj->rjk", inner, table, precision=lax.Precision.HIGHEST)
    transformed = outer.reshape(ROWS, N) / SIDE
    sketch = jnp.take(transformed, kept.astype(jnp.int32), axis=1).astype(jnp.bfloat16)
    widened = sketch.astype(jnp.float32)
    gram = jnp.dot(widened, widened.T, precision=lax.Precision.HIGHEST) / KEEP
    return gram.reshape(N_ROW, N_COL, ROW_DEV, ROWS)
```

```python
import functools

import jax
import jax.numpy as jnp
from jax import lax
from jax.experimental import pallas as pl
from jax.experimental.pallas import tpu as pltpu
from jax.sharding import PartitionSpec as P

LANES = 128
PACKED = 16
BUDGET = 40 * 1024 * 1024
MESH = pl.DeviceIdType.MESH
CONTRACT_LAST = (((1,), (1,)), ((), ()))


def signs_of(bits, dtype):
    return (1 - 2 * (lax.population_count(bits) & 1)).astype(jnp.float32).astype(dtype)


def fill_walsh(target, columns, first):
    depth, width = target.shape
    within = lax.broadcasted_iota(jnp.int32, (LANES, width), 0) + first
    blocks = [signs_of(within & columns, jnp.bfloat16)]
    step = LANES
    while step < depth:
        flip = jnp.broadcast_to(signs_of(columns & step, jnp.float32), (LANES, width)).astype(jnp.bfloat16)
        blocks = blocks + [block * flip for block in blocks]
        step *= 2
    for place, block in enumerate(blocks):
        target[pl.ds(place * LANES, LANES), :] = block


def sketch_kernel(
    n_col, n_row, theta_ref, signs_ref, kept_ref, out_ref,
    theta, walsh, parts, got, both, products, arrived,
    load_sem, part_send, part_recv, row_send, row_recv, gram_send, gram_recv,
):
    col, row = lax.axis_index("col"), lax.axis_index("row")
    rows, depth = theta.shape
    width = parts.shape[2]
    own = out_ref.shape[0]

    barrier = pltpu.get_barrier_semaphore()
    for step in range(1, n_col):
        pl.semaphore_signal(barrier, inc=1, device_id={"col": lax.rem(col + step, n_col)}, device_id_type=MESH)
    for step in range(1, n_row):
        pl.semaphore_signal(barrier, inc=1, device_id={"row": lax.rem(row + step, n_row)}, device_id_type=MESH)
    load = pltpu.make_async_copy(theta_ref, theta, load_sem)
    load.start()

    order = sorted(range(n_col), key=lambda step: -min(step, n_col - step))
    groups = [order[place:place + 2] for place in range(0, n_col, 2)]

    def columns_of(group):
        pieces = []
        for step in group:
            owner = lax.rem(col + step, n_col)
            pieces.append(kept_ref[:, pl.ds(pl.multiple_of(owner * width, LANES), width)])
        return jnp.concatenate(pieces, axis=1)

    first = col * depth
    fill_walsh(walsh.at[0], columns_of(groups[0]), first)
    flips = jnp.broadcast_to(signs_ref[...].astype(jnp.float32), (PACKED, depth)).astype(jnp.bfloat16)
    load.wait()
    for place in range(0, rows, PACKED):
        theta[pl.ds(place, PACKED), :] = theta[pl.ds(place, PACKED), :] * flips

    sends = []
    mine = None
    for place, group in enumerate(groups):
        if place:
            fill_walsh(walsh.at[place], columns_of(group), first)
        part = jnp.dot(theta[...], walsh[place], preferred_element_type=jnp.float32)
        if place == 0:
            pl.semaphore_wait(barrier, n_col + n_row - 2)
        for index, step in enumerate(group):
            piece = part[:, index * width:(index + 1) * width]
            if step == 0:
                mine = piece
                continue
            parts[step] = piece.astype(jnp.bfloat16)
            copy = pltpu.make_async_remote_copy(
                src_ref=parts.at[step], dst_ref=got.at[step],
                send_sem=part_send.at[step], recv_sem=part_recv.at[step],
                device_id={"col": lax.rem(col + step, n_col)}, device_id_type=MESH,
            )
            copy.start()
            sends.append((step, copy))

    total = mine
    for step, copy in reversed(sends):
        copy.wait_recv()
        total = total + got[step].astype(jnp.float32)
    sketch = total.astype(jnp.bfloat16)
    both[row] = sketch
    row_copies = []
    for step in range(1, n_row):
        copy = pltpu.make_async_remote_copy(
            src_ref=both.at[row], dst_ref=both.at[row],
            send_sem=row_send.at[step], recv_sem=row_recv.at[step],
            device_id={"row": lax.rem(row + step, n_row)}, device_id_type=MESH,
        )
        copy.start()
        row_copies.append(copy)
    for copy in row_copies:
        copy.wait_recv()
    everything = both[...].reshape(n_row * rows, width)
    gram = lax.dot_general(sketch, everything, CONTRACT_LAST, preferred_element_type=jnp.float32)
    products[...] = gram.astype(jnp.bfloat16).reshape(products.shape)
    gram_copies = []
    for step in order:
        if step == 0:
            continue
        owner = lax.rem(col + step, n_col)
        copy = pltpu.make_async_remote_copy(
            src_ref=products.at[owner], dst_ref=arrived.at[step],
            send_sem=gram_send.at[step], recv_sem=gram_recv.at[step],
            device_id={"col": owner}, device_id_type=MESH,
        )
        copy.start()
        gram_copies.append((step, copy))
    total = products[col].astype(jnp.float32)
    for step, copy in reversed(gram_copies):
        copy.wait_recv()
        total = total + arrived[step].astype(jnp.float32)
    scale = 1.0 / (n_col * depth * kept_ref.shape[1])
    out_ref[...] = total * scale
    for _, copy in sends + gram_copies:
        copy.wait_send()
    for copy in row_copies:
        copy.wait_send()


def fused(n_col, n_row, theta, signs, kept):
    rows, depth = theta.shape
    keep = kept.shape[0]
    width = keep // n_col
    own = rows // n_col
    bf16 = jnp.bfloat16
    dma = pltpu.SemaphoreType.DMA
    vmem = pl.BlockSpec(memory_space=pltpu.VMEM)
    gram = pl.pallas_call(
        functools.partial(sketch_kernel, n_col, n_row),
        out_shape=jax.ShapeDtypeStruct((own, n_row * rows), jnp.float32),
        in_specs=[pl.BlockSpec(memory_space=pl.ANY), vmem, vmem],
        out_specs=vmem,
        scratch_shapes=[
            pltpu.VMEM((rows, depth), bf16),
            pltpu.VMEM((n_col // 2, depth, 2 * width), bf16),
            pltpu.VMEM((n_col, rows, width), bf16),
            pltpu.VMEM((n_col, rows, width), bf16),
            pltpu.VMEM((n_row, rows, width), bf16),
            pltpu.VMEM((n_col, own, n_row * rows), bf16),
            pltpu.VMEM((n_col, own, n_row * rows), bf16),
            dma,
            dma((n_col,)), dma((n_col,)),
            dma((n_row,)), dma((n_row,)),
            dma((n_col,)), dma((n_col,)),
        ],
        compiler_params=pltpu.CompilerParams(
            collective_id=0, has_side_effects=True, vmem_limit_bytes=BUDGET
        ),
        cost_estimate=pl.CostEstimate(
            flops=2 * rows * depth * keep, bytes_accessed=2 * rows * depth, transcendentals=0
        ),
    )(theta, signs[None, :], kept[None, :])
    return gram.reshape(1, 1, own, n_row * rows)


def hadamard(order, dtype):
    indices = jnp.arange(order, dtype=jnp.int32)
    return signs_of(indices[:, None] & indices[None, :], dtype)


def gathered(n_col, side, theta, signs, kept):
    scaled = theta * signs.astype(jnp.bfloat16)[None, :]
    spread = lax.all_to_all(scaled, "col", split_axis=0, concat_axis=1, tiled=True)
    height = spread.shape[0]
    inner = jnp.dot(
        spread.reshape(height * side, side), hadamard(side, jnp.bfloat16), preferred_element_type=jnp.float32
    ).reshape(height, side, side)
    outer = jnp.einsum("rak,aj->rjk", inner, hadamard(side, jnp.float32), precision=lax.Precision.HIGHEST)
    transformed = outer.reshape(height, side * side) / side
    sketch = jnp.take(transformed, kept, axis=1).astype(jnp.bfloat16)
    half_rows = lax.all_gather(sketch, "col", axis=0, tiled=True)
    every = lax.all_gather(half_rows, "row", axis=0, tiled=True)
    gram = lax.dot_general(sketch, every, CONTRACT_LAST, preferred_element_type=jnp.float32)
    return gram / kept.shape[0]


def solution(mesh):
    n_col, n_row = mesh.shape["col"], mesh.shape["row"]

    def per_device(theta, signs, kept):
        rows, depth = theta.shape
        keep = kept.shape[0]
        aligned = keep % (n_col * LANES) == 0 and rows % (n_col * PACKED) == 0 and depth % LANES == 0
        held = 2 * (rows * depth + depth * keep + 3 * rows * keep + 4 * rows * n_row * rows)
        if aligned and n_col % 2 == 0 and 2 * held <= BUDGET:
            return fused(n_col, n_row, theta, signs, kept)
        columns = depth * n_col
        side = 1 << (columns.bit_length() - 1) // 2
        gram = gathered(n_col, side, theta, signs, kept)
        return gram[None, None]

    return jax.shard_map(
        per_device,
        mesh=mesh,
        in_specs=(P(("real", "row"), "col"), P(("real", "col")), P()),
        out_specs=P(("real", "row"), "col", None, None),
        check_vma=False,
    )
```

```python
import functools

import jax
import jax.numpy as jnp
from jax import lax
from jax.experimental import pallas as pl
from jax.experimental.pallas import tpu as pltpu
from jax.sharding import PartitionSpec as P

LANES = 128
PACKED = 16
BUDGET = 60 * 1024 * 1024
MESH = pl.DeviceIdType.MESH
CONTRACT_LAST = (((1,), (1,)), ((), ()))


def signs_of(bits, dtype):
    return (1 - 2 * (lax.population_count(bits) & 1)).astype(jnp.float32).astype(dtype)


def fill_walsh(target, columns, first):
    depth, width = target.shape
    within = lax.broadcasted_iota(jnp.int32, (LANES, width), 0) + first
    blocks = [signs_of(within & columns, jnp.bfloat16)]
    step = LANES
    while step < depth:
        flip = jnp.broadcast_to(signs_of(columns & step, jnp.float32), (LANES, width)).astype(jnp.bfloat16)
        blocks = blocks + [block * flip for block in blocks]
        step *= 2
    for place, block in enumerate(blocks):
        target[pl.ds(place * LANES, LANES), :] = block


def sketch_kernel(
    n_col, n_row, theta_in, signs_in, kept_in, out_ref,
    theta, signs_ref, kept_ref, walsh, parts, got, both, products, arrived,
    load_sem, part_send, part_recv, row_send, row_recv, gram_send, gram_recv,
):
    col, row = lax.axis_index("col"), lax.axis_index("row")
    rows, depth = theta.shape
    width = parts.shape[2]
    own = out_ref.shape[0]

    barrier = pltpu.get_barrier_semaphore()
    for step in range(1, n_col):
        pl.semaphore_signal(barrier, inc=1, device_id={"col": lax.rem(col + step, n_col)}, device_id_type=MESH)
    for step in range(1, n_row):
        pl.semaphore_signal(barrier, inc=1, device_id={"row": lax.rem(row + step, n_row)}, device_id_type=MESH)
    loads = [
        pltpu.make_async_copy(source, target, load_sem.at[place])
        for place, (source, target) in enumerate(((kept_in, kept_ref), (theta_in, theta), (signs_in, signs_ref)))
    ]
    for load in loads:
        load.start()

    order = sorted(range(n_col), key=lambda step: -min(step, n_col - step))
    groups = [order[place:place + 2] for place in range(0, n_col, 2)]

    def columns_of(group):
        pieces = []
        for step in group:
            owner = lax.rem(col + step, n_col)
            pieces.append(kept_ref[:, pl.ds(pl.multiple_of(owner * width, LANES), width)])
        return jnp.concatenate(pieces, axis=1)

    first = col * depth
    loads[0].wait()
    fill_walsh(walsh.at[0], columns_of(groups[0]), first)
    loads[2].wait()
    flips = jnp.broadcast_to(signs_ref[...].astype(jnp.float32), (PACKED, depth)).astype(jnp.bfloat16)
    loads[1].wait()
    for place in range(0, rows, PACKED):
        theta[pl.ds(place, PACKED), :] = theta[pl.ds(place, PACKED), :] * flips

    sends = []
    mine = None
    for place, group in enumerate(groups):
        if place:
            fill_walsh(walsh.at[place], columns_of(group), first)
        part = jnp.dot(theta[...], walsh[place], preferred_element_type=jnp.float32)
        if place == 0:
            pl.semaphore_wait(barrier, n_col + n_row - 2)
        for index, step in enumerate(group):
            piece = part[:, index * width:(index + 1) * width]
            if step == 0:
                mine = piece
                continue
            parts[step] = piece.astype(jnp.bfloat16)
            copy = pltpu.make_async_remote_copy(
                src_ref=parts.at[step], dst_ref=got.at[step],
                send_sem=part_send.at[step], recv_sem=part_recv.at[step],
                device_id={"col": lax.rem(col + step, n_col)}, device_id_type=MESH,
            )
            copy.start()
            sends.append((step, copy))

    total = mine
    for step, copy in reversed(sends):
        copy.wait_recv()
        total = total + got[step].astype(jnp.float32)
    sketch = total.astype(jnp.bfloat16)
    both[row] = sketch
    row_copies = []
    for step in range(1, n_row):
        copy = pltpu.make_async_remote_copy(
            src_ref=both.at[row], dst_ref=both.at[row],
            send_sem=row_send.at[step], recv_sem=row_recv.at[step],
            device_id={"row": lax.rem(row + step, n_row)}, device_id_type=MESH,
        )
        copy.start()
        row_copies.append(copy)
    for copy in row_copies:
        copy.wait_recv()
    everything = both[...].reshape(n_row * rows, width)
    gram = lax.dot_general(sketch, everything, CONTRACT_LAST, preferred_element_type=jnp.float32)
    products[...] = gram.astype(jnp.bfloat16).reshape(products.shape)
    gram_copies = []
    for step in order:
        if step == 0:
            continue
        owner = lax.rem(col + step, n_col)
        copy = pltpu.make_async_remote_copy(
            src_ref=products.at[owner], dst_ref=arrived.at[step],
            send_sem=gram_send.at[step], recv_sem=gram_recv.at[step],
            device_id={"col": owner}, device_id_type=MESH,
        )
        copy.start()
        gram_copies.append((step, copy))
    total = products[col].astype(jnp.float32)
    for step, copy in reversed(gram_copies):
        copy.wait_recv()
        total = total + arrived[step].astype(jnp.float32)
    scale = 1.0 / (n_col * depth * kept_ref.shape[1])
    out_ref[...] = total * scale
    for _, copy in sends + gram_copies:
        copy.wait_send()
    for copy in row_copies:
        copy.wait_send()


def fused(n_col, n_row, theta, signs, kept):
    rows, depth = theta.shape
    keep = kept.shape[0]
    width = keep // n_col
    own = rows // n_col
    bf16 = jnp.bfloat16
    dma = pltpu.SemaphoreType.DMA
    vmem = pl.BlockSpec(memory_space=pltpu.VMEM)
    gram = pl.pallas_call(
        functools.partial(sketch_kernel, n_col, n_row),
        out_shape=jax.ShapeDtypeStruct((own, n_row * rows), jnp.float32),
        in_specs=[pl.BlockSpec(memory_space=pltpu.HBM)] * 3,
        out_specs=vmem,
        scratch_shapes=[
            pltpu.VMEM((rows, depth), bf16),
            pltpu.VMEM((1, depth), jnp.int32),
            pltpu.VMEM((1, keep), jnp.int32),
            pltpu.VMEM((n_col // 2, depth, 2 * width), bf16),
            pltpu.VMEM((n_col, rows, width), bf16),
            pltpu.VMEM((n_col, rows, width), bf16),
            pltpu.VMEM((n_row, rows, width), bf16),
            pltpu.VMEM((n_col, own, n_row * rows), bf16),
            pltpu.VMEM((n_col, own, n_row * rows), bf16),
            dma((3,)),
            dma((n_col,)), dma((n_col,)),
            dma((n_row,)), dma((n_row,)),
            dma((n_col,)), dma((n_col,)),
        ],
        compiler_params=pltpu.CompilerParams(
            collective_id=0, has_side_effects=True, vmem_limit_bytes=BUDGET
        ),
        cost_estimate=pl.CostEstimate(
            flops=2 * rows * depth * keep, bytes_accessed=2 * rows * depth, transcendentals=0
        ),
    )(theta, signs[None, :], kept[None, :])
    return gram.reshape(1, 1, own, n_row * rows)


def hadamard(order, dtype):
    indices = jnp.arange(order, dtype=jnp.int32)
    return signs_of(indices[:, None] & indices[None, :], dtype)


def gathered(n_col, side, theta, signs, kept):
    scaled = theta * signs.astype(jnp.bfloat16)[None, :]
    spread = lax.all_to_all(scaled, "col", split_axis=0, concat_axis=1, tiled=True)
    height = spread.shape[0]
    inner = jnp.dot(
        spread.reshape(height * side, side), hadamard(side, jnp.bfloat16), preferred_element_type=jnp.float32
    ).reshape(height, side, side)
    outer = jnp.einsum("rak,aj->rjk", inner, hadamard(side, jnp.float32), precision=lax.Precision.HIGHEST)
    transformed = outer.reshape(height, side * side) / side
    sketch = jnp.take(transformed, kept, axis=1).astype(jnp.bfloat16)
    half_rows = lax.all_gather(sketch, "col", axis=0, tiled=True)
    every = lax.all_gather(half_rows, "row", axis=0, tiled=True)
    gram = lax.dot_general(sketch, every, CONTRACT_LAST, preferred_element_type=jnp.float32)
    return gram / kept.shape[0]


def solution(mesh):
    n_col, n_row = mesh.shape["col"], mesh.shape["row"]

    def per_device(theta, signs, kept):
        rows, depth = theta.shape
        keep = kept.shape[0]
        aligned = keep % (n_col * LANES) == 0 and rows % (n_col * PACKED) == 0 and depth % LANES == 0
        held = 2 * (rows * depth + depth * keep + 3 * rows * keep + 4 * rows * n_row * rows)
        if aligned and n_col % 2 == 0 and 2 * held <= BUDGET:
            return fused(n_col, n_row, theta, signs, kept)
        columns = depth * n_col
        side = 1 << (columns.bit_length() - 1) // 2
        gram = gathered(n_col, side, theta, signs, kept)
        return gram[None, None]

    return jax.shard_map(
        per_device,
        mesh=mesh,
        in_specs=(P(("real", "row"), "col"), P(("real", "col")), P()),
        out_specs=P(("real", "row"), "col", None, None),
        check_vma=False,
    )
```

```python
import functools

import jax
import jax.numpy as jnp
from jax import lax
from jax.experimental import pallas as pl
from jax.experimental.pallas import tpu as pltpu
from jax.sharding import PartitionSpec as P

LANES = 128
PACKED = 16
BUDGET = 40 * 1024 * 1024
MESH = pl.DeviceIdType.MESH
CONTRACT_LAST = (((1,), (1,)), ((), ()))


def signs_of(bits, dtype):
    return (1 - 2 * (lax.population_count(bits) & 1)).astype(jnp.float32).astype(dtype)


def fill_walsh(target, columns, first):
    depth, width = target.shape
    within = lax.broadcasted_iota(jnp.int32, (LANES, width), 0) + first
    blocks = [signs_of(within & columns, jnp.bfloat16)]
    step = LANES
    while step < depth:
        flip = jnp.broadcast_to(signs_of(columns & step, jnp.float32), (LANES, width)).astype(jnp.bfloat16)
        blocks = blocks + [block * flip for block in blocks]
        step *= 2
    for place, block in enumerate(blocks):
        target[pl.ds(place * LANES, LANES), :] = block


def sketch_kernel(
    n_col, n_row, theta_in, signs_in, kept_in, out_ref,
    theta, signs_ref, kept_ref, walsh, parts, got, both, products, arrived,
    load_sem, part_send, part_recv, row_send, row_recv, gram_send, gram_recv,
):
    col, row = lax.axis_index("col"), lax.axis_index("row")
    rows, depth = theta.shape
    width = parts.shape[2]
    own = out_ref.shape[0]

    barrier = pltpu.get_barrier_semaphore()
    for step in range(1, n_col):
        pl.semaphore_signal(barrier, inc=1, device_id={"col": lax.rem(col + step, n_col)}, device_id_type=MESH)
    for step in range(1, n_row):
        pl.semaphore_signal(barrier, inc=1, device_id={"row": lax.rem(row + step, n_row)}, device_id_type=MESH)
    loads = [
        pltpu.make_async_copy(source, target, load_sem.at[place])
        for place, (source, target) in enumerate(((kept_in, kept_ref), (theta_in, theta), (signs_in, signs_ref)))
    ]
    for load in loads:
        load.start()

    order = sorted(range(n_col), key=lambda step: -min(step, n_col - step))
    groups = [order[place:place + 2] for place in range(0, n_col, 2)]

    def columns_of(group):
        pieces = []
        for step in group:
            owner = lax.rem(col + step, n_col)
            pieces.append(kept_ref[:, pl.ds(pl.multiple_of(owner * width, LANES), width)])
        return jnp.concatenate(pieces, axis=1)

    first = col * depth
    loads[0].wait()
    fill_walsh(walsh.at[0], columns_of(groups[0]), first)
    loads[2].wait()
    flips = jnp.broadcast_to(signs_ref[...].astype(jnp.float32), (PACKED, depth)).astype(jnp.bfloat16)
    loads[1].wait()
    for place in range(0, rows, PACKED):
        theta[pl.ds(place, PACKED), :] = theta[pl.ds(place, PACKED), :] * flips

    sends = []
    mine = None
    for place, group in enumerate(groups):
        if place:
            fill_walsh(walsh.at[place], columns_of(group), first)
        part = jnp.dot(theta[...], walsh[place], preferred_element_type=jnp.float32)
        if place == 0:
            pl.semaphore_wait(barrier, n_col + n_row - 2)
        for index, step in enumerate(group):
            piece = part[:, index * width:(index + 1) * width]
            if step == 0:
                mine = piece
                continue
            parts[step] = piece.astype(jnp.bfloat16)
            copy = pltpu.make_async_remote_copy(
                src_ref=parts.at[step], dst_ref=got.at[step],
                send_sem=part_send.at[step], recv_sem=part_recv.at[step],
                device_id={"col": lax.rem(col + step, n_col)}, device_id_type=MESH,
            )
            copy.start()
            sends.append((step, copy))

    total = mine
    for step, copy in reversed(sends):
        copy.wait_recv()
        total = total + got[step].astype(jnp.float32)
    sketch = total.astype(jnp.bfloat16)
    both[row] = sketch
    row_copies = []
    for step in range(1, n_row):
        copy = pltpu.make_async_remote_copy(
            src_ref=both.at[row], dst_ref=both.at[row],
            send_sem=row_send.at[step], recv_sem=row_recv.at[step],
            device_id={"row": lax.rem(row + step, n_row)}, device_id_type=MESH,
        )
        copy.start()
        row_copies.append(copy)
    for copy in row_copies:
        copy.wait_recv()
    everything = both[...].reshape(n_row * rows, width)
    gram = lax.dot_general(sketch, everything, CONTRACT_LAST, preferred_element_type=jnp.float32)
    products[...] = gram.astype(jnp.bfloat16).reshape(products.shape)
    gram_copies = []
    for step in order:
        if step == 0:
            continue
        owner = lax.rem(col + step, n_col)
        copy = pltpu.make_async_remote_copy(
            src_ref=products.at[owner], dst_ref=arrived.at[step],
            send_sem=gram_send.at[step], recv_sem=gram_recv.at[step],
            device_id={"col": owner}, device_id_type=MESH,
        )
        copy.start()
        gram_copies.append((step, copy))
    total = products[col].astype(jnp.float32)
    for step, copy in reversed(gram_copies):
        copy.wait_recv()
        total = total + arrived[step].astype(jnp.float32)
    scale = 1.0 / (n_col * depth * kept_ref.shape[1])
    out_ref[...] = total * scale
    for _, copy in sends + gram_copies:
        copy.wait_send()
    for copy in row_copies:
        copy.wait_send()


def fused(n_col, n_row, theta, signs, kept):
    rows, depth = theta.shape
    keep = kept.shape[0]
    width = keep // n_col
    own = rows // n_col
    bf16 = jnp.bfloat16
    dma = pltpu.SemaphoreType.DMA
    vmem = pl.BlockSpec(memory_space=pltpu.VMEM)
    gram = pl.pallas_call(
        functools.partial(sketch_kernel, n_col, n_row),
        out_shape=jax.ShapeDtypeStruct((own, n_row * rows), jnp.float32),
        in_specs=[pl.BlockSpec(memory_space=pltpu.HBM)] * 3,
        out_specs=vmem,
        scratch_shapes=[
            pltpu.VMEM((rows, depth), bf16),
            pltpu.VMEM((1, depth), jnp.int32),
            pltpu.VMEM((1, keep), jnp.int32),
            pltpu.VMEM((n_col // 2, depth, 2 * width), bf16),
            pltpu.VMEM((n_col, rows, width), bf16),
            pltpu.VMEM((n_col, rows, width), bf16),
            pltpu.VMEM((n_row, rows, width), bf16),
            pltpu.VMEM((n_col, own, n_row * rows), bf16),
            pltpu.VMEM((n_col, own, n_row * rows), bf16),
            dma((3,)),
            dma((n_col,)), dma((n_col,)),
            dma((n_row,)), dma((n_row,)),
            dma((n_col,)), dma((n_col,)),
        ],
        compiler_params=pltpu.CompilerParams(
            collective_id=0, has_side_effects=True, vmem_limit_bytes=BUDGET
        ),
        cost_estimate=pl.CostEstimate(
            flops=2 * rows * depth * keep, bytes_accessed=2 * rows * depth, transcendentals=0
        ),
    )(*[pltpu.with_memory_space_constraint(each, pltpu.HBM) for each in (theta, signs[None, :], kept[None, :])])
    return gram.reshape(1, 1, own, n_row * rows)


def hadamard(order, dtype):
    indices = jnp.arange(order, dtype=jnp.int32)
    return signs_of(indices[:, None] & indices[None, :], dtype)


def gathered(n_col, side, theta, signs, kept):
    scaled = theta * signs.astype(jnp.bfloat16)[None, :]
    spread = lax.all_to_all(scaled, "col", split_axis=0, concat_axis=1, tiled=True)
    height = spread.shape[0]
    inner = jnp.dot(
        spread.reshape(height * side, side), hadamard(side, jnp.bfloat16), preferred_element_type=jnp.float32
    ).reshape(height, side, side)
    outer = jnp.einsum("rak,aj->rjk", inner, hadamard(side, jnp.float32), precision=lax.Precision.HIGHEST)
    transformed = outer.reshape(height, side * side) / side
    sketch = jnp.take(transformed, kept, axis=1).astype(jnp.bfloat16)
    half_rows = lax.all_gather(sketch, "col", axis=0, tiled=True)
    every = lax.all_gather(half_rows, "row", axis=0, tiled=True)
    gram = lax.dot_general(sketch, every, CONTRACT_LAST, preferred_element_type=jnp.float32)
    return gram / kept.shape[0]


def solution(mesh):
    n_col, n_row = mesh.shape["col"], mesh.shape["row"]

    def per_device(theta, signs, kept):
        rows, depth = theta.shape
        keep = kept.shape[0]
        aligned = keep % (n_col * LANES) == 0 and rows % (n_col * PACKED) == 0 and depth % LANES == 0
        held = 2 * (rows * depth + depth * keep + 3 * rows * keep + 4 * rows * n_row * rows)
        if aligned and n_col % 2 == 0 and 2 * held <= BUDGET:
            return fused(n_col, n_row, theta, signs, kept)
        columns = depth * n_col
        side = 1 << (columns.bit_length() - 1) // 2
        gram = gathered(n_col, side, theta, signs, kept)
        return gram[None, None]

    return jax.shard_map(
        per_device,
        mesh=mesh,
        in_specs=(P(("real", "row"), "col"), P(("real", "col")), P()),
        out_specs=P(("real", "row"), "col", None, None),
        check_vma=False,
    )
```
